256 devices in a mesh: img: 32 (over z, x_hi, core), sp: 8 (over x_lo, y).
Axes of the slice: x: 4 (x_hi: 2, x_lo: 2; x = x_hi * 2 + x_lo), y: 4, z: 8, core: 2. Of those that a mesh axis runs over, the one named last changes fastest.
Arguments:
- fresh_qkv: bfloat16 [65536, 9216], P(('img', 'sp')), parts along dimension 0, may hold values from -8 to 8
- stale_kv: bfloat16 [65536, 6144], P(('img', 'sp')), parts along dimension 0, may hold values from -8 to 8
- stale_out: bfloat16 [65536, 3072], P(('img', 'sp')), parts along dimension 0, may hold values from -3 to 3
- edit_count: int32 [256], P(('img', 'sp')), parts along dimension 0, may hold values from 0 to 256, as said below
- edit_rows: int32 [65536], P(('img', 'sp')), parts along dimension 0, may hold values from 0 to 255, as said below
Outputs:
- attention_out: bfloat16 [65536, 3072], P(('img', 'sp')), parts along dimension 0
The draws below stay inside these ranges and needn't reach their ends.
There are 32 independent parts, one for each index of `img`. The reference program is written for one: setup_inputs(seed, part) draws one part's arguments, and reference() takes and returns one part's arrays. A program takes and returns all parts, laid end to end along the dimension named above; each array names one. Nothing has to cross between parts.
Inputs may be any that keep to these rules, and one draw needn't show every extreme that they name: `edit_count`: within each image the counts sum to at most 1536, and one index of sp has exactly 256. `edit_rows`: each block of 256 entries (one index of sp) is a permutation of 0 to 255.
All inputs are finite; a program needn't handle non-finite values.
Results may differ from the reference program's by a relative error of at most 0.004.
Values may be sent and summed in bfloat16 or wider, within the bound.
A program may use at most 192 MiB of HBM per device.

```python
import jax
import jax.numpy as jnp
from jax import lax

HEADS = 24
HEAD_DIM = 128
D = 3072
TOK_DEV = 256
TOKENS = 2048
WORK = 192


def base_values(key, columns, spread):
    raw = jnp.clip(jax.random.normal(key, (TOKENS, columns), jnp.float32), -4.5, 4.5)
    return raw * spread


def draw_fresh_qkv(key, part):
    key = jax.random.fold_in(key, 11)
    base_key = jax.random.fold_in(key, 0)
    spread = jnp.concatenate([jnp.full((2 * D,), 1.6, jnp.float32), jnp.full((D,), 1.0, jnp.float32)])
    values = base_values(base_key, 3 * D, spread)
    return values.astype(jnp.bfloat16)


def draw_stale_kv(key, part):
    key = jax.random.fold_in(key, 13)
    spread = jnp.concatenate([jnp.full((D,), 1.6, jnp.float32), jnp.full((D,), 1.0, jnp.float32)])
    values = base_values(key, 2 * D, spread)
    return values.astype(jnp.bfloat16)


def draw_edit_count(key, part):
    key = jax.random.fold_in(key, 7)
    groups = TOKENS // TOK_DEV
    others = groups - 1
    remaining = groups * WORK - TOK_DEV
    room = min(TOK_DEV, remaining // others)
    count_key, place_key = jax.random.split(key, 2)
    counts = jax.random.randint(count_key, (others,), 0, room + 1)
    full_counts = jnp.concatenate([jnp.full((1,), TOK_DEV, jnp.int32), counts.astype(jnp.int32)])
    placing = jax.random.permutation(place_key, groups)
    return full_counts[placing].astype(jnp.int32)


def draw_edit_rows(key, part):
    key = jax.random.fold_in(key, 5)
    groups = TOKENS // TOK_DEV
    keys = jax.random.split(key, groups)
    lists = jax.vmap(lambda single: jax.random.permutation(single, TOK_DEV))(keys)
    return lists.reshape(TOKENS).astype(jnp.int32)


def block_levels(stream_key, dims, cuts, smallest, high):
    factor_of, own = 1.0, jax.random.fold_in(stream_key, 6)
    for axis_at, blocks in cuts:
        heights = jnp.exp(jax.random.uniform(jax.random.fold_in(own, axis_at), (blocks,), jnp.float32, smallest / len(cuts), high / len(cuts)))
        factor_of = factor_of * jnp.repeat(heights, dims[axis_at] // blocks).reshape([-1 if axis == axis_at else 1 for axis in range(len(dims))])
    return factor_of


def scatter_about(own_key, dims, deviation, reach, pieces=(), kind=jnp.bfloat16):
    result = deviation * jax.random.normal(own_key, dims, jnp.float32)
    if pieces:
        result = result * block_levels(own_key, dims, pieces, -0.22, 0.18)
    return jnp.clip(result, -reach, reach).astype(kind)


def setup_inputs(seed: int = 0, part: int = 0) -> dict:
    splits = jax.random.split(jax.random.key(seed), 6)
    part_splits = jax.random.split(jax.random.fold_in(splits[5], part), 6)
    fresh_qkv = draw_fresh_qkv(jax.random.fold_in(jax.random.fold_in(splits[5], part), 71), part)
    stale_kv = draw_stale_kv(jax.random.fold_in(jax.random.fold_in(splits[5], part), 71), part)
    stale_out = scatter_about(part_splits[2], (TOKENS, D), 0.5, 3.0, ((0, 8),))
    edit_count = draw_edit_count(jax.random.fold_in(jax.random.fold_in(splits[5], part), 71), part)
    edit_rows = draw_edit_rows(jax.random.fold_in(jax.random.fold_in(splits[5], part), 71), part)
    return dict(fresh_qkv=fresh_qkv, stale_kv=stale_kv, stale_out=stale_out, edit_count=edit_count, edit_rows=edit_rows)


def reference(fresh_qkv, stale_kv, stale_out, edit_count, edit_rows):
    groups = TOKENS // TOK_DEV
    row_lists = edit_rows.reshape(groups, TOK_DEV)
    slot_iota = jnp.arange(TOK_DEV, dtype=jnp.int32)
    live_slots = slot_iota[None, :] < edit_count[:, None]
    matches = (row_lists[:, :, None] == slot_iota[None, None, :]) & live_slots[:, :, None]
    edited = jnp.any(matches, axis=1).reshape(TOKENS)
    merged = jnp.where(edited[:, None], fresh_qkv[:, D:], stale_kv)
    queries = fresh_qkv[:, :D]
    score_scale = HEAD_DIM ** -0.5

    def per_head(index):
        start = (index * HEAD_DIM).astype(jnp.int32)
        query_part = lax.dynamic_slice_in_dim(queries, start, HEAD_DIM, 1)
        key_part = lax.dynamic_slice_in_dim(merged, start, HEAD_DIM, 1)
        value_part = lax.dynamic_slice_in_dim(merged, (start + D).astype(jnp.int32), HEAD_DIM, 1)
        scores = jnp.dot(query_part, key_part.T, preferred_element_type=jnp.float32) * score_scale
        peaks = jnp.max(scores, axis=1, keepdims=True)
        weights = jnp.exp(scores - peaks)
        totals = jnp.sum(weights, axis=1, keepdims=True)
        summed = jnp.dot(weights.astype(jnp.bfloat16), value_part, preferred_element_type=jnp.float32)
        return summed / totals

    stacked = lax.map(per_head, jnp.arange(HEADS, dtype=jnp.int32))
    attended = jnp.transpose(stacked, (1, 0, 2)).reshape(TOKENS, D).astype(jnp.bfloat16)
    return jnp.where(edited[:, None], attended, stale_out)
```

```python
import functools

import jax
import jax.numpy as jnp
from jax import lax
from jax.experimental import pallas as pl
from jax.experimental.pallas import tpu as pltpu
from jax.sharding import PartitionSpec as P

HEADS = 24
HEAD_DIM = 128
EXP2_SCALE = HEAD_DIM ** (-0.5) * 1.4426950408889634
RING = 4
PEERS = ((1, 0), (0, 1), (0, 3), (1, 2), (1, 1), (1, 3), (0, 2))


def cols(index):
    return pl.ds(pl.multiple_of(index * HEAD_DIM, HEAD_DIM), HEAD_DIM)


def kernel(
    n,
    heads_own,
    count_ref,
    rows_ref,
    fresh,
    stale,
    att,
    mask_ref,
    fresh_kv,
    stale_kv,
    rows_vmem,
    outbox,
    q_all,
    kv_all,
    o_all,
    load_sem,
    q_send,
    q_recv,
    kv_send,
    kv_recv,
    o_send,
    o_recv,
):
    me = lax.axis_index("sp")
    tok = fresh.shape[0]
    width = fresh.shape[1] // 3

    def rows(index):
        return pl.ds(pl.multiple_of(index * tok, tok), tok)

    def peer(step):
        over, along = step
        return lax.rem(me // RING + over, 2) * RING + lax.rem(lax.rem(me, RING) + along, RING)

    rows_load = pltpu.make_async_copy(rows_ref, rows_vmem, load_sem.at[2, 0])
    rows_load.start()
    loads = []
    for part in range(2):
        at = pl.ds(part * width, width)
        loads.append(
            (
                pltpu.make_async_copy(
                    fresh.at[:, pl.ds((part + 1) * width, width)], fresh_kv.at[:, at], load_sem.at[part, 0]
                ),
                pltpu.make_async_copy(stale.at[:, at], stale_kv.at[:, at], load_sem.at[part, 1]),
            )
        )
    for pair in loads:
        for load in pair:
            load.start()

    barrier = pltpu.get_barrier_semaphore()

    for step in PEERS:
        pl.semaphore_signal(
            barrier, inc=1, device_id={"sp": peer(step)}, device_id_type=pl.DeviceIdType.MESH
        )
    pl.semaphore_wait(barrier, n - 1)

    def q_copy(j, dest):
        return pltpu.make_async_remote_copy(
            src_ref=fresh.at[:, cols(dest * heads_own + j)],
            dst_ref=q_all.at[j, rows(me)],
            send_sem=q_send.at[j, dest],
            recv_sem=q_recv.at[j, me],
            device_id={"sp": dest},
            device_id_type=pl.DeviceIdType.MESH,
        )

    def q_own(j):
        return pltpu.make_async_copy(
            fresh.at[:, cols(me * heads_own + j)], q_all.at[j, rows(me)], q_recv.at[j, me]
        )

    def kv_copy(j, dest):
        return pltpu.make_async_remote_copy(
            src_ref=outbox.at[j, dest],
            dst_ref=kv_all.at[j, :, rows(me)],
            send_sem=kv_send.at[j, dest],
            recv_sem=kv_recv.at[j, me],
            device_id={"sp": dest},
            device_id_type=pl.DeviceIdType.MESH,
        )

    def kv_own(j):
        return pltpu.make_async_copy(outbox.at[j, me], kv_all.at[j, :, rows(me)], kv_recv.at[j, me])

    def o_copy(j, dest):
        return pltpu.make_async_remote_copy(
            src_ref=o_all.at[j, rows(dest)],
            dst_ref=att.at[:, cols(me * heads_own + j)],
            send_sem=o_send.at[j, dest],
            recv_sem=o_recv.at[j, me],
            device_id={"sp": dest},
            device_id_type=pl.DeviceIdType.MESH,
        )

    def o_own(j):
        return pltpu.make_async_copy(
            o_all.at[j, rows(me)], att.at[:, cols(me * heads_own + j)], o_recv.at[j, me]
        )

    def send_q(j):
        for step in PEERS:
            q_copy(j, peer(step)).start()
        q_own(j).start()

    def merge(j, dest, mask):
        for part in range(2):
            at = cols(part * HEADS + dest * heads_own + j)
            outbox[j, dest, part] = jnp.where(
                mask, fresh_kv[:, at].astype(jnp.float32), stale_kv[:, at].astype(jnp.float32)
            ).astype(jnp.bfloat16)

    def send_kv(j):
        mask = mask_ref[...] > 0.0
        for step in PEERS:
            merge(j, peer(step), mask)
            kv_copy(j, peer(step)).start()
        merge(j, me, mask)
        kv_own(j).start()

    def wait_q(j, source):
        pltpu.make_async_copy(
            q_all.at[j, rows(source)], q_all.at[j, rows(source)], q_recv.at[j, source]
        ).wait()

    def wait_kv(j, source):
        pltpu.make_async_copy(
            kv_all.at[j, :, rows(source)], kv_all.at[j, :, rows(source)], kv_recv.at[j, source]
        ).wait()

    send_q(0)

    rows_load.wait()
    slot = lax.broadcasted_iota(jnp.int32, (1, tok), 1)
    live = jnp.where(slot < count_ref[0], rows_vmem[...], -1)
    hit = lax.broadcasted_iota(jnp.int32, (tok, tok), 0) == live
    edited = jnp.max(hit.astype(jnp.float32), axis=1, keepdims=True)
    mask_ref[...] = jnp.broadcast_to(edited, (tok, HEAD_DIM))

    for pair in loads:
        for load in pair:
            load.wait()

    send_kv(0)

    def enqueue(j, carry):
        send_kv(j)
        send_q(j)
        return carry

    lax.fori_loop(1, heads_own, enqueue, 0)

    def head(j, carry):
        for step in ((0, 0),) + PEERS:
            wait_kv(j, peer(step))

        def block(index, carry):
            dest = lax.rem(me + index, n)
            wait_q(j, dest)
            scores = lax.dot_general(
                q_all[j, rows(dest)],
                kv_all[j, 0],
                (((1,), (1,)), ((), ())),
                preferred_element_type=jnp.float32,
            )
            top = jnp.max(scores, axis=1, keepdims=True)
            weights = jnp.exp2((scores - top) * EXP2_SCALE)
            total = jnp.sum(weights, axis=1, keepdims=True)
            summed = jnp.dot(
                weights.astype(jnp.bfloat16), kv_all[j, 1], preferred_element_type=jnp.float32
            )
            o_all[j, rows(dest)] = (summed / total).astype(jnp.bfloat16)

            @pl.when(index > 0)
            def _():
                o_copy(j, dest).start()

            @pl.when(index == 0)
            def _():
                o_own(j).start()

            return carry

        lax.fori_loop(0, n, block, 0)
        return carry

    lax.fori_loop(0, heads_own, head, 0)

    def drain(j, carry):
        for step in PEERS:
            q_copy(j, peer(step)).wait_send()
            kv_copy(j, peer(step)).wait_send()
            o_copy(j, peer(step)).wait_send()
        for step in ((0, 0),) + PEERS:
            at = cols(peer(step) * heads_own + j)
            pltpu.make_async_copy(att.at[:, at], att.at[:, at], o_recv.at[j, peer(step)]).wait()
        return carry

    lax.fori_loop(0, heads_own, drain, 0)


def on_device(n, fresh_qkv, stale_kv, stale_out, edit_count, edit_rows):
    tok, width = stale_out.shape
    heads_own = HEADS // n
    total = tok * n
    flops = heads_own * total * total * HEAD_DIM * 4
    bf16 = jnp.bfloat16
    sems = pltpu.SemaphoreType.DMA((heads_own, n))
    att, mask = pl.pallas_call(
        functools.partial(kernel, n, heads_own),
        out_shape=(
            jax.ShapeDtypeStruct((tok, width), bf16),
            jax.ShapeDtypeStruct((tok, HEAD_DIM), jnp.float32),
        ),
        in_specs=[
            pl.BlockSpec(memory_space=pltpu.SMEM),
            pl.BlockSpec(memory_space=pltpu.HBM),
            pl.BlockSpec(memory_space=pltpu.HBM),
            pl.BlockSpec(memory_space=pltpu.HBM),
        ],
        out_specs=(pl.BlockSpec(memory_space=pl.ANY), pl.BlockSpec(memory_space=pltpu.VMEM)),
        scratch_shapes=[
            pltpu.VMEM((tok, 2 * width), bf16),
            pltpu.VMEM((tok, 2 * width), bf16),
            pltpu.VMEM((1, tok), jnp.int32),
            pltpu.VMEM((heads_own, n, 2, tok, HEAD_DIM), bf16),
            pltpu.VMEM((heads_own, total, HEAD_DIM), bf16),
            pltpu.VMEM((heads_own, 2, total, HEAD_DIM), bf16),
            pltpu.VMEM((heads_own, total, HEAD_DIM), bf16),
            pltpu.SemaphoreType.DMA((3, 2)),
            sems,
            sems,
            sems,
            sems,
            sems,
            sems,
        ],
        compiler_params=pltpu.CompilerParams(
            collective_id=0, has_side_effects=True, vmem_limit_bytes=48 * 1024 * 1024
        ),
        cost_estimate=pl.CostEstimate(
            flops=flops, bytes_accessed=8 * tok * width * 2, transcendentals=heads_own * total * total
        ),
    )(
        edit_count,
        pltpu.with_memory_space_constraint(edit_rows.reshape(1, tok), pltpu.HBM),
        pltpu.with_memory_space_constraint(fresh_qkv, pltpu.HBM),
        pltpu.with_memory_space_constraint(stale_kv, pltpu.HBM),
    )
    return jnp.where(mask[:, :1] > 0.0, att, stale_out)


def solution(mesh):
    n = mesh.shape["sp"]
    spec = P(("img", "sp"), None)
    flat = P(("img", "sp"))
    return jax.shard_map(
        functools.partial(on_device, n),
        mesh=mesh,
        in_specs=(spec, spec, spec, flat, flat),
        out_specs=spec,
        check_vma=False,
    )
```

```python
import functools

import jax
import jax.numpy as jnp
from jax import lax
from jax.experimental import pallas as pl
from jax.experimental.pallas import tpu as pltpu
from jax.sharding import PartitionSpec as P

HEADS = 24
HEAD_DIM = 128
EXP2_SCALE = HEAD_DIM ** (-0.5) * 1.4426950408889634
RING = 4
BLOCKS = 4
CHUNK = 16
PEERS = ((1, 2), (0, 2), (1, 1), (1, 3), (0, 1), (0, 3), (1, 0))


def cols(index):
    return pl.ds(pl.multiple_of(index * HEAD_DIM, HEAD_DIM), HEAD_DIM)


def kernel(
    n,
    heads_own,
    count_ref,
    rows_ref,
    fresh,
    stale,
    stale_out,
    out_ref,
    att,
    mask_ref,
    fresh_kv,
    stale_kv,
    rows_vmem,
    outbox,
    q_all,
    kv_all,
    o_all,
    scores,
    probs,
    load_sem,
    q_send,
    q_recv,
    kv_send,
    kv_recv,
    o_send,
    o_recv,
):
    me = lax.axis_index("sp")
    tok = fresh.shape[0]
    width = fresh.shape[1] // 3

    def rows(index):
        return pl.ds(pl.multiple_of(index * tok, tok), tok)

    turn_of = 1 + 2 * lax.rem(lax.axis_index("img"), 2)

    def peer(step):
        over, along = step
        return lax.rem(me // RING + over, 2) * RING + lax.rem(lax.rem(me, RING) + along * turn_of, RING)

    rows_load = pltpu.make_async_copy(rows_ref, rows_vmem, load_sem.at[2, 0])
    rows_load.start()
    out_load = pltpu.make_async_copy(stale_out, out_ref, load_sem.at[2, 1])
    loads = []
    for part in range(2):
        at = pl.ds(part * width, width)
        loads.append(
            (
                pltpu.make_async_copy(
                    fresh.at[:, pl.ds((part + 1) * width, width)], fresh_kv.at[:, at], load_sem.at[part, 0]
                ),
                pltpu.make_async_copy(stale.at[:, at], stale_kv.at[:, at], load_sem.at[part, 1]),
            )
        )
    for pair in loads:
        for load in pair:
            load.start()

    barrier = pltpu.get_barrier_semaphore()

    for step in PEERS:
        pl.semaphore_signal(
            barrier, inc=1, device_id={"sp": peer(step)}, device_id_type=pl.DeviceIdType.MESH
        )
    pl.semaphore_wait(barrier, n - 1)

    def q_copy(j, dest):
        return pltpu.make_async_remote_copy(
            src_ref=fresh.at[:, cols(dest * heads_own + j)],
            dst_ref=q_all.at[j, rows(me)],
            send_sem=q_send.at[j, dest],
            recv_sem=q_recv.at[j, me],
            device_id={"sp": dest},
            device_id_type=pl.DeviceIdType.MESH,
        )

    def q_own(j):
        return pltpu.make_async_copy(
            fresh.at[:, cols(me * heads_own + j)], q_all.at[j, rows(me)], q_recv.at[j, me]
        )

    def kv_copy(j, dest):
        return pltpu.make_async_remote_copy(
            src_ref=outbox.at[j, dest],
            dst_ref=kv_all.at[j, :, rows(me)],
            send_sem=kv_send.at[j, dest],
            recv_sem=kv_recv.at[j, me],
            device_id={"sp": dest},
            device_id_type=pl.DeviceIdType.MESH,
        )

    def kv_own(j):
        return pltpu.make_async_copy(outbox.at[j, me], kv_all.at[j, :, rows(me)], kv_recv.at[j, me])

    def o_copy(j, dest):
        return pltpu.make_async_remote_copy(
            src_ref=o_all.at[j, rows(dest)],
            dst_ref=att.at[:, cols(me * heads_own + j)],
            send_sem=o_send.at[j, dest],
            recv_sem=o_recv.at[j, me],
            device_id={"sp": dest},
            device_id_type=pl.DeviceIdType.MESH,
        )

    def o_own(j):
        return pltpu.make_async_copy(
            o_all.at[j, rows(me)], att.at[:, cols(me * heads_own + j)], o_recv.at[j, me]
        )

    def send_q(j):
        for step in PEERS:
            q_copy(j, peer(step)).start()
        q_own(j).start()

    def merge(j, dest, mask):
        for part in range(2):
            at = cols(part * HEADS + dest * heads_own + j)
            outbox[j, dest, part] = jnp.where(
                mask, fresh_kv[:, at].astype(jnp.float32), stale_kv[:, at].astype(jnp.float32)
            ).astype(jnp.bfloat16)

    def send_kv(j):
        mask = mask_ref[...] > 0.0
        for step in PEERS:
            merge(j, peer(step), mask)
            kv_copy(j, peer(step)).start()
        merge(j, me, mask)
        kv_own(j).start()

    def wait_q(j, source):
        pltpu.make_async_copy(
            q_all.at[j, rows(source)], q_all.at[j, rows(source)], q_recv.at[j, source]
        ).wait()

    def wait_kv(j, source):
        pltpu.make_async_copy(
            kv_all.at[j, :, rows(source)], kv_all.at[j, :, rows(source)], kv_recv.at[j, source]
        ).wait()

    send_q(0)

    rows_load.wait()
    slot = lax.broadcasted_iota(jnp.int32, (1, tok), 1)
    live = jnp.where(slot < count_ref[0], rows_vmem[...], -1)
    hit = lax.broadcasted_iota(jnp.int32, (tok, tok), 0) == live
    edited = jnp.max(hit.astype(jnp.float32), axis=1, keepdims=True)
    mask_ref[...] = jnp.broadcast_to(edited, (tok, HEAD_DIM))

    for pair in loads:
        for load in pair:
            load.wait()

    def sent_q(j):
        for step in PEERS:
            q_copy(j, peer(step)).wait_send()

    def sent_kv(j):
        for step in PEERS:
            kv_copy(j, peer(step)).wait_send()

    out_load.start()
    send_kv(0)
    sent_q(0)
    send_kv(1)
    sent_kv(0)
    send_q(1)

    def score(j, dest, slot):
        scores[slot] = lax.dot_general(
            q_all[j, rows(dest)],
            kv_all[j, 0],
            (((1,), (1,)), ((), ())),
            preferred_element_type=jnp.float32,
        )

    def soften(slot):
        for first in range(0, tok, CHUNK):
            piece = scores[slot, first : first + CHUNK]
            top = jnp.max(piece, axis=1, keepdims=True)
            probs[slot, first : first + CHUNK] = jnp.exp2((piece - top) * EXP2_SCALE).astype(jnp.bfloat16)

    def gather(j, dest, slot):
        values = kv_all[j, 1]
        summed = jnp.dot(
            probs[slot],
            jnp.concatenate([values, jnp.ones_like(values)], axis=1),
            preferred_element_type=jnp.float32,
        )
        o_all[j, rows(dest)] = (summed[:, :HEAD_DIM] / summed[:, HEAD_DIM:]).astype(jnp.bfloat16)

    order = PEERS + ((0, 0),)

    def send_o(j, step):
        if step == (0, 0):
            o_own(j).start()
        else:
            o_copy(j, peer(step)).start()

    def head(j, carry):
        @pl.when(j > 0)
        def _():
            sent_kv(j)

            @pl.when(j + 1 < heads_own)
            def _():
                send_kv(j + 1)

            sent_q(j)

            @pl.when(j + 1 < heads_own)
            def _():
                send_q(j + 1)

        @pl.when(j + 1 == heads_own)
        def _():
            def early(before, carry):
                for step in order:
                    send_o(before, step)
                return carry

            lax.fori_loop(0, heads_own - 1, early, 0)

        for step in order:
            wait_kv(j, peer(step))
            wait_q(j, peer(step))

        for first in range(0, n, BLOCKS):
            steps = order[first : first + BLOCKS]
            score(j, peer(steps[0]), 0)
            for index, step in enumerate(steps):
                if index + 1 < BLOCKS:
                    score(j, peer(steps[index + 1]), (index + 1) % 2)
                soften(index % 2)
                gather(j, peer(step), index % 2)

            @pl.when(j + 1 == heads_own)
            def _():
                for step in steps:
                    send_o(j, step)

        return carry

    lax.fori_loop(0, heads_own, head, 0)

    out_load.wait()

    def drain(j, carry):
        mask = mask_ref[...] > 0.0
        for step in PEERS[::-1] + ((0, 0),):
            at = cols(peer(step) * heads_own + j)
            pltpu.make_async_copy(att.at[:, at], att.at[:, at], o_recv.at[j, peer(step)]).wait()
            out_ref[:, at] = jnp.where(
                mask, att[:, at].astype(jnp.float32), out_ref[:, at].astype(jnp.float32)
            ).astype(jnp.bfloat16)
        for step in PEERS:
            o_copy(j, peer(step)).wait_send()
        return carry

    lax.fori_loop(0, heads_own, drain, 0)


def on_device(n, fresh_qkv, stale_kv, stale_out, edit_count, edit_rows):
    tok, width = stale_out.shape
    heads_own = HEADS // n
    total = tok * n
    flops = heads_own * total * total * HEAD_DIM * 4
    bf16 = jnp.bfloat16
    sems = pltpu.SemaphoreType.DMA((heads_own, n))
    return pl.pallas_call(
        functools.partial(kernel, n, heads_own),
        out_shape=jax.ShapeDtypeStruct((tok, width), bf16),
        in_specs=[
            pl.BlockSpec(memory_space=pltpu.SMEM),
            pl.BlockSpec(memory_space=pltpu.HBM),
            pl.BlockSpec(memory_space=pltpu.HBM),
            pl.BlockSpec(memory_space=pltpu.HBM),
            pl.BlockSpec(memory_space=pltpu.HBM),
        ],
        out_specs=pl.BlockSpec(memory_space=pltpu.VMEM),
        scratch_shapes=[
            pltpu.VMEM((tok, width), bf16),
            pltpu.VMEM((tok, HEAD_DIM), jnp.float32),
            pltpu.VMEM((tok, 2 * width), bf16),
            pltpu.VMEM((tok, 2 * width), bf16),
            pltpu.VMEM((1, tok), jnp.int32),
            pltpu.VMEM((heads_own, n, 2, tok, HEAD_DIM), bf16),
            pltpu.VMEM((heads_own, total, HEAD_DIM), bf16),
            pltpu.VMEM((heads_own, 2, total, HEAD_DIM), bf16),
            pltpu.VMEM((heads_own, total, HEAD_DIM), bf16),
            pltpu.VMEM((2, tok, total), jnp.float32),
            pltpu.VMEM((2, tok, total), bf16),
            pltpu.SemaphoreType.DMA((3, 2)),
            sems,
            sems,
            sems,
            sems,
            sems,
            sems,
        ],
        compiler_params=pltpu.CompilerParams(
            collective_id=0, has_side_effects=True, vmem_limit_bytes=48 * 1024 * 1024
        ),
        cost_estimate=pl.CostEstimate(
            flops=flops, bytes_accessed=8 * tok * width * 2, transcendentals=heads_own * total * total
        ),
    )(
        edit_count,
        pltpu.with_memory_space_constraint(edit_rows.reshape(1, tok), pltpu.HBM),
        pltpu.with_memory_space_constraint(fresh_qkv, pltpu.HBM),
        pltpu.with_memory_space_constraint(stale_kv, pltpu.HBM),
        pltpu.with_memory_space_constraint(stale_out, pltpu.HBM),
    )


def solution(mesh):
    n = mesh.shape["sp"]
    spec = P(("img", "sp"), None)
    flat = P(("img", "sp"))
    return jax.shard_map(
        functools.partial(on_device, n),
        mesh=mesh,
        in_specs=(spec, spec, spec, flat, flat),
        out_specs=spec,
        check_vma=False,
    )
```

```python
import functools

import jax
import jax.numpy as jnp
from jax import lax
from jax.experimental import pallas as pl
from jax.experimental.pallas import tpu as pltpu
from jax.sharding import PartitionSpec as P

HEADS = 24
HEAD_DIM = 128
EXP2_SCALE = HEAD_DIM ** (-0.5) * 1.4426950408889634
RING = 4
BLOCKS = 4
CHUNK = 16
PEERS = ((1, 2), (0, 2), (1, 1), (1, 3), (0, 1), (0, 3), (1, 0))


def cols(index):
    return pl.ds(pl.multiple_of(index * HEAD_DIM, HEAD_DIM), HEAD_DIM)


def kernel(
    n,
    heads_own,
    count_ref,
    rows_ref,
    fresh,
    stale,
    stale_out,
    out_ref,
    att,
    mask_ref,
    fresh_kv,
    stale_kv,
    rows_vmem,
    outbox,
    q_all,
    kv_all,
    o_all,
    scores,
    probs,
    load_sem,
    q_send,
    q_recv,
    kv_send,
    kv_recv,
    o_send,
    o_recv,
):
    me = lax.axis_index("sp")
    tok = fresh.shape[0]
    width = fresh.shape[1] // 3

    def rows(index):
        return pl.ds(pl.multiple_of(index * tok, tok), tok)

    turn_of = 1 + 2 * lax.rem(lax.axis_index("img"), 2)

    def peer(step):
        over, along = step
        return lax.rem(me // RING + over, 2) * RING + lax.rem(lax.rem(me, RING) + along * turn_of, RING)

    barrier = pltpu.get_barrier_semaphore()

    for step in PEERS:
        pl.semaphore_signal(
            barrier, inc=1, device_id={"sp": peer(step)}, device_id_type=pl.DeviceIdType.MESH
        )
    rows_load = pltpu.make_async_copy(rows_ref, rows_vmem, load_sem.at[2, 0])
    rows_load.start()
    out_load = pltpu.make_async_copy(stale_out, out_ref, load_sem.at[2, 1])
    loads = []
    for part in range(2):
        at = pl.ds(part * width, width)
        loads.append(
            (
                pltpu.make_async_copy(
                    fresh.at[:, pl.ds((part + 1) * width, width)], fresh_kv.at[:, at], load_sem.at[part, 0]
                ),
                pltpu.make_async_copy(stale.at[:, at], stale_kv.at[:, at], load_sem.at[part, 1]),
            )
        )
    for pair in loads:
        for load in pair:
            load.start()

    pl.semaphore_wait(barrier, n - 1)

    def q_copy(j, dest):
        return pltpu.make_async_remote_copy(
            src_ref=fresh.at[:, cols(dest * heads_own + j)],
            dst_ref=q_all.at[j, rows(me)],
            send_sem=q_send.at[j, dest],
            recv_sem=q_recv.at[j, me],
            device_id={"sp": dest},
            device_id_type=pl.DeviceIdType.MESH,
        )

    def q_own(j):
        return pltpu.make_async_copy(
            fresh.at[:, cols(me * heads_own + j)], q_all.at[j, rows(me)], q_recv.at[j, me]
        )

    def kv_copy(j, dest):
        return pltpu.make_async_remote_copy(
            src_ref=outbox.at[j, dest],
            dst_ref=kv_all.at[j, :, rows(me)],
            send_sem=kv_send.at[j, dest],
            recv_sem=kv_recv.at[j, me],
            device_id={"sp": dest},
            device_id_type=pl.DeviceIdType.MESH,
        )

    def kv_own(j):
        return pltpu.make_async_copy(outbox.at[j, me], kv_all.at[j, :, rows(me)], kv_recv.at[j, me])

    def o_copy(j, dest):
        return pltpu.make_async_remote_copy(
            src_ref=o_all.at[j, rows(dest)],
            dst_ref=att.at[:, cols(me * heads_own + j)],
            send_sem=o_send.at[j, dest],
            recv_sem=o_recv.at[j, me],
            device_id={"sp": dest},
            device_id_type=pl.DeviceIdType.MESH,
        )

    def o_own(j):
        return pltpu.make_async_copy(
            o_all.at[j, rows(me)], att.at[:, cols(me * heads_own + j)], o_recv.at[j, me]
        )

    def send_q(j):
        for step in PEERS:
            q_copy(j, peer(step)).start()
        q_own(j).start()

    def merge(j, dest, mask):
        for part in range(2):
            at = cols(part * HEADS + dest * heads_own + j)
            outbox[j, dest, part] = jnp.where(
                mask, fresh_kv[:, at].astype(jnp.float32), stale_kv[:, at].astype(jnp.float32)
            ).astype(jnp.bfloat16)

    def send_kv(j):
        mask = mask_ref[...] > 0.0
        for step in PEERS:
            merge(j, peer(step), mask)
            kv_copy(j, peer(step)).start()
        merge(j, me, mask)
        kv_own(j).start()

    def wait_q(j, source):
        pltpu.make_async_copy(
            q_all.at[j, rows(source)], q_all.at[j, rows(source)], q_recv.at[j, source]
        ).wait()

    def wait_kv(j, source):
        pltpu.make_async_copy(
            kv_all.at[j, :, rows(source)], kv_all.at[j, :, rows(source)], kv_recv.at[j, source]
        ).wait()

    send_q(0)

    rows_load.wait()
    slot = lax.broadcasted_iota(jnp.int32, (1, tok), 1)
    live = jnp.where(slot < count_ref[0], rows_vmem[...], -1)
    hit = lax.broadcasted_iota(jnp.int32, (tok, tok), 0) == live
    edited = jnp.max(hit.astype(jnp.float32), axis=1, keepdims=True)
    mask_ref[...] = jnp.broadcast_to(edited, (tok, HEAD_DIM))

    for pair in loads:
        for load in pair:
            load.wait()

    def sent_q(j):
        for step in PEERS:
            q_copy(j, peer(step)).wait_send()

    def sent_kv(j):
        for step in PEERS:
            kv_copy(j, peer(step)).wait_send()

    out_load.start()
    send_kv(0)

    def enqueue(j, carry):
        send_kv(j)
        send_q(j)
        return carry

    lax.fori_loop(1, heads_own, enqueue, 0)

    def score(j, dest, slot):
        scores[slot] = lax.dot_general(
            q_all[j, rows(dest)],
            kv_all[j, 0],
            (((1,), (1,)), ((), ())),
            preferred_element_type=jnp.float32,
        )

    def soften(slot):
        for first in range(0, tok, CHUNK):
            piece = scores[slot, first : first + CHUNK]
            top = jnp.max(piece, axis=1, keepdims=True)
            probs[slot, first : first + CHUNK] = jnp.exp2((piece - top) * EXP2_SCALE).astype(jnp.bfloat16)

    def gather(j, dest, slot):
        values = kv_all[j, 1]
        summed = jnp.dot(
            probs[slot],
            jnp.concatenate([values, jnp.ones_like(values)], axis=1),
            preferred_element_type=jnp.float32,
        )
        o_all[j, rows(dest)] = (summed[:, :HEAD_DIM] / summed[:, HEAD_DIM:]).astype(jnp.bfloat16)

    order = PEERS + ((0, 0),)

    def send_o(j, step):
        if step == (0, 0):
            o_own(j).start()
        else:
            o_copy(j, peer(step)).start()

    def head(j, carry, last=False):
        for step in order:
            wait_kv(j, peer(step))
            wait_q(j, peer(step))

        for first in range(0, n, BLOCKS):
            steps = order[first : first + BLOCKS]
            score(j, peer(steps[0]), 0)
            for index, step in enumerate(steps):
                if index + 1 < BLOCKS:
                    score(j, peer(steps[index + 1]), (index + 1) % 2)
                soften(index % 2)
                gather(j, peer(step), index % 2)
                if last:
                    send_o(j, step)

        return carry

    def outputs(j, carry):
        for step in order:
            send_o(j, step)
        return carry

    def sent(j, carry):
        sent_kv(j)
        sent_q(j)
        return carry

    final = heads_own - 1
    lax.fori_loop(0, final, head, 0)
    lax.fori_loop(0, final, sent, 0)
    sent_kv(final)
    lax.fori_loop(0, final - 1, outputs, 0)
    sent_q(final)
    outputs(final - 1, 0)
    head(final, 0, last=True)

    out_load.wait()

    def drain(j, carry):
        mask = mask_ref[...] > 0.0
        for step in PEERS[::-1] + ((0, 0),):
            at = cols(peer(step) * heads_own + j)
            pltpu.make_async_copy(att.at[:, at], att.at[:, at], o_recv.at[j, peer(step)]).wait()
            out_ref[:, at] = jnp.where(
                mask, att[:, at].astype(jnp.float32), out_ref[:, at].astype(jnp.float32)
            ).astype(jnp.bfloat16)
        for step in PEERS:
            o_copy(j, peer(step)).wait_send()
        return carry

    lax.fori_loop(0, heads_own, drain, 0)


def on_device(n, fresh_qkv, stale_kv, stale_out, edit_count, edit_rows):
    tok, width = stale_out.shape
    heads_own = HEADS // n
    total = tok * n
    flops = heads_own * total * total * HEAD_DIM * 4
    bf16 = jnp.bfloat16
    sems = pltpu.SemaphoreType.DMA((heads_own, n))
    return pl.pallas_call(
        functools.partial(kernel, n, heads_own),
        out_shape=jax.ShapeDtypeStruct((tok, width), bf16),
        in_specs=[
            pl.BlockSpec(memory_space=pltpu.SMEM),
            pl.BlockSpec(memory_space=pltpu.HBM),
            pl.BlockSpec(memory_space=pltpu.HBM),
            pl.BlockSpec(memory_space=pltpu.HBM),
            pl.BlockSpec(memory_space=pltpu.HBM),
        ],
        out_specs=pl.BlockSpec(memory_space=pltpu.VMEM),
        scratch_shapes=[
            pltpu.VMEM((tok, width), bf16),
            pltpu.VMEM((tok, HEAD_DIM), jnp.float32),
            pltpu.VMEM((tok, 2 * width), bf16),
            pltpu.VMEM((tok, 2 * width), bf16),
            pltpu.VMEM((1, tok), jnp.int32),
            pltpu.VMEM((heads_own, n, 2, tok, HEAD_DIM), bf16),
            pltpu.VMEM((heads_own, total, HEAD_DIM), bf16),
            pltpu.VMEM((heads_own, 2, total, HEAD_DIM), bf16),
            pltpu.VMEM((heads_own, total, HEAD_DIM), bf16),
            pltpu.VMEM((2, tok, total), jnp.float32),
            pltpu.VMEM((2, tok, total), bf16),
            pltpu.SemaphoreType.DMA((3, 2)),
            sems,
            sems,
            sems,
            sems,
            sems,
            sems,
        ],
        compiler_params=pltpu.CompilerParams(
            collective_id=0, has_side_effects=True, vmem_limit_bytes=48 * 1024 * 1024
        ),
        cost_estimate=pl.CostEstimate(
            flops=flops, bytes_accessed=8 * tok * width * 2, transcendentals=heads_own * total * total
        ),
    )(
        edit_count,
        pltpu.with_memory_space_constraint(edit_rows.reshape(1, tok), pltpu.HBM),
        pltpu.with_memory_space_constraint(fresh_qkv, pltpu.HBM),
        pltpu.with_memory_space_constraint(stale_kv, pltpu.HBM),
        pltpu.with_memory_space_constraint(stale_out, pltpu.HBM),
    )


def solution(mesh):
    n = mesh.shape["sp"]
    spec = P(("img", "sp"), None)
    flat = P(("img", "sp"))
    return jax.shard_map(
        functools.partial(on_device, n),
        mesh=mesh,
        in_specs=(spec, spec, spec, flat, flat),
        out_specs=spec,
        check_vma=False,
    )
```

```python
import functools

import jax
import jax.numpy as jnp
from jax import lax
from jax.experimental import pallas as pl
from jax.experimental.pallas import tpu as pltpu
from jax.sharding import PartitionSpec as P

HEADS = 24
HEAD_DIM = 128
EXP2_SCALE = HEAD_DIM ** (-0.5) * 1.4426950408889634
RING = 4
BLOCKS = 4
CHUNK = 16
PEERS = ((1, 2), (0, 2), (1, 1), (1, 3), (0, 1), (0, 3), (1, 0))


def cols(index):
    return pl.ds(pl.multiple_of(index * HEAD_DIM, HEAD_DIM), HEAD_DIM)


def kernel(
    n,
    heads_own,
    count_ref,
    rows_ref,
    fresh,
    stale,
    stale_out,
    out_ref,
    att,
    mask_ref,
    fresh_kv,
    stale_kv,
    rows_vmem,
    q_box,
    stage_sem,
    outbox,
    q_all,
    kv_all,
    o_all,
    scores,
    probs,
    load_sem,
    q_send,
    q_recv,
    kv_send,
    kv_recv,
    o_send,
    o_recv,
):
    me = lax.axis_index("sp")
    tok = fresh.shape[0]
    width = fresh.shape[1] // 3

    def rows(index):
        return pl.ds(pl.multiple_of(index * tok, tok), tok)

    turn_of = 1 + 2 * lax.rem(lax.axis_index("img"), 2)

    def peer(step):
        over, along = step
        return lax.rem(me // RING + over, 2) * RING + lax.rem(lax.rem(me, RING) + along * turn_of, RING)

    barrier = pltpu.get_barrier_semaphore()

    for step in PEERS:
        pl.semaphore_signal(
            barrier, inc=1, device_id={"sp": peer(step)}, device_id_type=pl.DeviceIdType.MESH
        )
    rows_load = pltpu.make_async_copy(rows_ref, rows_vmem, load_sem.at[2, 0])
    rows_load.start()
    out_load = pltpu.make_async_copy(stale_out, out_ref, load_sem.at[2, 1])
    loads = []
    for part in range(2):
        at = pl.ds(part * width, width)
        loads.append(
            (
                pltpu.make_async_copy(
                    fresh.at[:, pl.ds((part + 1) * width, width)], fresh_kv.at[:, at], load_sem.at[part, 0]
                ),
                pltpu.make_async_copy(stale.at[:, at], stale_kv.at[:, at], load_sem.at[part, 1]),
            )
        )
    pl.semaphore_wait(barrier, n - 1)

    def q_source(j, dest):
        if isinstance(j, int) and j == 0:
            return fresh.at[:, cols(dest * heads_own)]
        return q_box.at[j - 1, dest]

    def q_copy(j, dest):
        return pltpu.make_async_remote_copy(
            src_ref=q_source(j, dest),
            dst_ref=q_all.at[j, rows(me)],
            send_sem=q_send.at[j, dest],
            recv_sem=q_recv.at[j, me],
            device_id={"sp": dest},
            device_id_type=pl.DeviceIdType.MESH,
        )

    def q_own(j):
        return pltpu.make_async_copy(q_source(j, me), q_all.at[j, rows(me)], q_recv.at[j, me])

    def kv_copy(j, dest):
        return pltpu.make_async_remote_copy(
            src_ref=outbox.at[j, dest],
            dst_ref=kv_all.at[j, :, rows(me)],
            send_sem=kv_send.at[j, dest],
            recv_sem=kv_recv.at[j, me],
            device_id={"sp": dest},
            device_id_type=pl.DeviceIdType.MESH,
        )

    def kv_own(j):
        return pltpu.make_async_copy(outbox.at[j, me], kv_all.at[j, :, rows(me)], kv_recv.at[j, me])

    def o_copy(j, dest):
        return pltpu.make_async_remote_copy(
            src_ref=o_all.at[j, rows(dest)],
            dst_ref=att.at[me * heads_own + j],
            send_sem=o_send.at[j, dest],
            recv_sem=o_recv.at[j, me],
            device_id={"sp": dest},
            device_id_type=pl.DeviceIdType.MESH,
        )

    def o_own(j):
        return pltpu.make_async_copy(
            o_all.at[j, rows(me)], att.at[me * heads_own + j], o_recv.at[j, me]
        )

    def send_q(j):
        for step in PEERS:
            q_copy(j, peer(step)).start()
        q_own(j).start()

    def merge(j, dest, mask):
        for part in range(2):
            at = cols(part * HEADS + dest * heads_own + j)
            outbox[j, dest, part] = jnp.where(
                mask, fresh_kv[:, at].astype(jnp.float32), stale_kv[:, at].astype(jnp.float32)
            ).astype(jnp.bfloat16)

    def send_kv(j):
        mask = mask_ref[...] > 0.0
        for step in PEERS:
            merge(j, peer(step), mask)
            kv_copy(j, peer(step)).start()
        merge(j, me, mask)
        kv_own(j).start()

    def wait_q(j, source):
        pltpu.make_async_copy(
            q_all.at[j, rows(source)], q_all.at[j, rows(source)], q_recv.at[j, source]
        ).wait()

    def wait_kv(j, source):
        pltpu.make_async_copy(
            kv_all.at[j, :, rows(source)], kv_all.at[j, :, rows(source)], kv_recv.at[j, source]
        ).wait()

    send_q(0)
    for pair in loads:
        for load in pair:
            load.start()
    stages = [
        pltpu.make_async_copy(fresh.at[:, cols(dest * heads_own + j)], q_box.at[j - 1, dest], stage_sem.at[j - 1, dest])
        for j in range(1, heads_own)
        for dest in range(n)
    ]
    for stage in stages:
        stage.start()

    rows_load.wait()
    slot = lax.broadcasted_iota(jnp.int32, (1, tok), 1)
    live = jnp.where(slot < count_ref[0], rows_vmem[...], -1)
    hit = lax.broadcasted_iota(jnp.int32, (tok, tok), 0) == live
    edited = jnp.max(hit.astype(jnp.float32), axis=1, keepdims=True)
    mask_ref[...] = jnp.broadcast_to(edited, (tok, HEAD_DIM))

    for pair in loads:
        for load in pair:
            load.wait()

    def sent_q(j):
        for step in PEERS:
            q_copy(j, peer(step)).wait_send()

    def sent_kv(j):
        for step in PEERS:
            kv_copy(j, peer(step)).wait_send()

    out_load.start()
    send_kv(0)
    sent_q(0)
    for stage in stages:
        stage.wait()
    send_kv(1)
    sent_kv(0)
    send_q(1)

    def score(j, dest, slot):
        scores[slot] = lax.dot_general(
            q_all[j, rows(dest)],
            kv_all[j, 0],
            (((1,), (1,)), ((), ())),
            preferred_element_type=jnp.float32,
        )

    def soften(slot):
        for first in range(0, tok, CHUNK):
            piece = scores[slot, first : first + CHUNK]
            top = jnp.max(piece, axis=1, keepdims=True)
            probs[slot, first : first + CHUNK] = jnp.exp2((piece - top) * EXP2_SCALE).astype(jnp.bfloat16)

    def gather(j, dest, slot):
        values = kv_all[j, 1]
        summed = jnp.dot(
            probs[slot],
            jnp.concatenate([values, jnp.ones_like(values)], axis=1),
            preferred_element_type=jnp.float32,
        )
        o_all[j, rows(dest)] = (summed[:, :HEAD_DIM] / summed[:, HEAD_DIM:]).astype(jnp.bfloat16)

    order = PEERS + ((0, 0),)

    def send_o(j, step):
        if step == (0, 0):
            o_own(j).start()
        else:
            o_copy(j, peer(step)).start()

    def head(j, carry):
        @pl.when(j > 0)
        def _():
            sent_kv(j)

            @pl.when(j + 1 < heads_own)
            def _():
                send_kv(j + 1)

            sent_q(j)

            @pl.when(j + 1 < heads_own)
            def _():
                send_q(j + 1)

        @pl.when(j + 1 == heads_own)
        def _():
            def early(before, carry):
                for step in order:
                    send_o(before, step)
                return carry

            lax.fori_loop(0, heads_own - 1, early, 0)

        for step in order:
            wait_kv(j, peer(step))
            wait_q(j, peer(step))

        for first in range(0, n, BLOCKS):
            steps = order[first : first + BLOCKS]
            score(j, peer(steps[0]), 0)
            for index, step in enumerate(steps):
                if index + 1 < BLOCKS:
                    score(j, peer(steps[index + 1]), (index + 1) % 2)
                soften(index % 2)
                gather(j, peer(step), index % 2)

            @pl.when(j + 1 == heads_own)
            def _():
                for step in steps:
                    send_o(j, step)

        return carry

    lax.fori_loop(0, heads_own, head, 0)

    out_load.wait()

    def drain(j, carry):
        mask = mask_ref[...] > 0.0
        for step in PEERS[::-1] + ((0, 0),):
            index = peer(step) * heads_own + j
            at = cols(index)
            pltpu.make_async_copy(att.at[index], att.at[index], o_recv.at[j, peer(step)]).wait()
            out_ref[:, at] = jnp.where(
                mask, att[index].astype(jnp.float32), out_ref[:, at].astype(jnp.float32)
            ).astype(jnp.bfloat16)
        for step in PEERS:
            o_copy(j, peer(step)).wait_send()
        return carry

    lax.fori_loop(0, heads_own, drain, 0)


def on_device(n, fresh_qkv, stale_kv, stale_out, edit_count, edit_rows):
    tok, width = stale_out.shape
    heads_own = HEADS // n
    total = tok * n
    flops = heads_own * total * total * HEAD_DIM * 4
    bf16 = jnp.bfloat16
    sems = pltpu.SemaphoreType.DMA((heads_own, n))
    return pl.pallas_call(
        functools.partial(kernel, n, heads_own),
        out_shape=jax.ShapeDtypeStruct((tok, width), bf16),
        in_specs=[
            pl.BlockSpec(memory_space=pltpu.SMEM),
            pl.BlockSpec(memory_space=pltpu.HBM),
            pl.BlockSpec(memory_space=pltpu.HBM),
            pl.BlockSpec(memory_space=pltpu.HBM),
            pl.BlockSpec(memory_space=pltpu.HBM),
        ],
        out_specs=pl.BlockSpec(memory_space=pltpu.VMEM),
        scratch_shapes=[
            pltpu.VMEM((HEADS, tok, HEAD_DIM), bf16),
            pltpu.VMEM((tok, HEAD_DIM), jnp.float32),
            pltpu.VMEM((tok, 2 * width), bf16),
            pltpu.VMEM((tok, 2 * width), bf16),
            pltpu.VMEM((1, tok), jnp.int32),
            pltpu.VMEM((heads_own - 1, n, tok, HEAD_DIM), bf16),
            pltpu.SemaphoreType.DMA((heads_own - 1, n)),
            pltpu.VMEM((heads_own, n, 2, tok, HEAD_DIM), bf16),
            pltpu.VMEM((heads_own, total, HEAD_DIM), bf16),
            pltpu.VMEM((heads_own, 2, total, HEAD_DIM), bf16),
            pltpu.VMEM((heads_own, total, HEAD_DIM), bf16),
            pltpu.VMEM((2, tok, total), jnp.float32),
            pltpu.VMEM((2, tok, total), bf16),
            pltpu.SemaphoreType.DMA((3, 2)),
            sems,
            sems,
            sems,
            sems,
            sems,
            sems,
        ],
        compiler_params=pltpu.CompilerParams(
            collective_id=0, has_side_effects=True, vmem_limit_bytes=48 * 1024 * 1024
        ),
        cost_estimate=pl.CostEstimate(
            flops=flops, bytes_accessed=8 * tok * width * 2, transcendentals=heads_own * total * total
        ),
    )(
        edit_count,
        pltpu.with_memory_space_constraint(edit_rows.reshape(1, tok), pltpu.HBM),
        pltpu.with_memory_space_constraint(fresh_qkv, pltpu.HBM),
        pltpu.with_memory_space_constraint(stale_kv, pltpu.HBM),
        pltpu.with_memory_space_constraint(stale_out, pltpu.HBM),
    )


def solution(mesh):
    n = mesh.shape["sp"]
    spec = P(("img", "sp"), None)
    flat = P(("img", "sp"))
    return jax.shard_map(
        functools.partial(on_device, n),
        mesh=mesh,
        in_specs=(spec, spec, spec, flat, flat),
        out_specs=spec,
        check_vma=False,
    )
```

```python
import functools

import jax
import jax.numpy as jnp
from jax import lax
from jax.experimental import pallas as pl
from jax.experimental.pallas import tpu as pltpu
from jax.sharding import PartitionSpec as P

HEADS = 24
HEAD_DIM = 128
EXP2_SCALE = HEAD_DIM ** (-0.5) * 1.4426950408889634
RING = 4
BLOCKS = 4
CHUNK = 16
SLABS = 8
ORDERS = (
    ((1, 2), (0, 2), (1, 1), (0, 1), (1, 3), (0, 3), (1, 0)),
    ((0, 2), (1, 2), (0, 3), (1, 3), (0, 1), (1, 1), (1, 0)),
)


def cols(index):
    return pl.ds(pl.multiple_of(index * HEAD_DIM, HEAD_DIM), HEAD_DIM)


def kernel(
    n,
    heads_own,
    count_ref,
    rows_ref,
    fresh,
    stale,
    stale_out,
    out_ref,
    att,
    mask_ref,
    fresh_kv,
    stale_kv,
    rows_vmem,
    q_box,
    stage_sem,
    outbox,
    q_all,
    kv_all,
    o_all,
    scores,
    probs,
    load_sem,
    q_send,
    q_recv,
    kv_send,
    kv_recv,
    o_send,
    o_recv,
):
    me = lax.axis_index("sp")
    tok = fresh.shape[0]
    width = fresh.shape[1] // 3

    def rows(index):
        return pl.ds(pl.multiple_of(index * tok, tok), tok)

    def device_at(step):
        over, along = step
        return lax.rem(me // RING + over, 2) * RING + lax.rem(lax.rem(me, RING) + along, RING)

    first_core = lax.rem(lax.axis_index("img"), 2) == 0
    peers = [jnp.where(first_core, device_at(one), device_at(other)) for one, other in zip(*ORDERS)]

    barrier = pltpu.get_barrier_semaphore()

    for dest in peers:
        pl.semaphore_signal(barrier, inc=1, device_id={"sp": dest}, device_id_type=pl.DeviceIdType.MESH)
    rows_load = pltpu.make_async_copy(rows_ref, rows_vmem, load_sem.at[2, 0])
    rows_load.start()
    out_load = pltpu.make_async_copy(stale_out, out_ref, load_sem.at[2, 1])
    loads = []
    for part in range(2):
        at = pl.ds(part * width, width)
        loads.append(
            (
                pltpu.make_async_copy(
                    fresh.at[:, pl.ds((part + 1) * width, width)], fresh_kv.at[:, at], load_sem.at[part, 0]
                ),
                pltpu.make_async_copy(stale.at[:, at], stale_kv.at[:, at], load_sem.at[part, 1]),
            )
        )
    pl.semaphore_wait(barrier, n - 1)

    def q_source(j, dest):
        if isinstance(j, int) and j == 0:
            return fresh.at[:, cols(dest * heads_own)]
        return q_box.at[j - 1, dest]

    def q_copy(j, dest):
        return pltpu.make_async_remote_copy(
            src_ref=q_source(j, dest),
            dst_ref=q_all.at[j, rows(me)],
            send_sem=q_send.at[j, dest],
            recv_sem=q_recv.at[j, me],
            device_id={"sp": dest},
            device_id_type=pl.DeviceIdType.MESH,
        )

    def q_own(j):
        return pltpu.make_async_copy(q_source(j, me), q_all.at[j, rows(me)], q_recv.at[j, me])

    def kv_copy(j, dest):
        return pltpu.make_async_remote_copy(
            src_ref=outbox.at[j, dest],
            dst_ref=kv_all.at[j, :, rows(me)],
            send_sem=kv_send.at[j, dest],
            recv_sem=kv_recv.at[j, me],
            device_id={"sp": dest},
            device_id_type=pl.DeviceIdType.MESH,
        )

    def kv_own(j):
        return pltpu.make_async_copy(outbox.at[j, me], kv_all.at[j, :, rows(me)], kv_recv.at[j, me])

    def o_copy(j, dest):
        return pltpu.make_async_remote_copy(
            src_ref=o_all.at[j, rows(dest)],
            dst_ref=att.at[me * heads_own + j],
            send_sem=o_send.at[j, dest],
            recv_sem=o_recv.at[j, me],
            device_id={"sp": dest},
            device_id_type=pl.DeviceIdType.MESH,
        )

    def o_own(j):
        return pltpu.make_async_copy(
            o_all.at[j, rows(me)], att.at[me * heads_own + j], o_recv.at[j, me]
        )

    def send_q(j):
        for dest in peers:
            q_copy(j, dest).start()
        q_own(j).start()

    def merge(j, dest, mask):
        for part in range(2):
            at = cols(part * HEADS + dest * heads_own + j)
            outbox[j, dest, part] = jnp.where(
                mask, fresh_kv[:, at].astype(jnp.float32), stale_kv[:, at].astype(jnp.float32)
            ).astype(jnp.bfloat16)

    def send_kv(j):
        mask = mask_ref[...] > 0.0
        for dest in peers:
            merge(j, dest, mask)
            kv_copy(j, dest).start()
        merge(j, me, mask)
        kv_own(j).start()

    def wait_q(j, source):
        pltpu.make_async_copy(
            q_all.at[j, rows(source)], q_all.at[j, rows(source)], q_recv.at[j, source]
        ).wait()

    def wait_kv(j, source):
        pltpu.make_async_copy(
            kv_all.at[j, :, rows(source)], kv_all.at[j, :, rows(source)], kv_recv.at[j, source]
        ).wait()

    send_q(0)
    for pair in loads:
        for load in pair:
            load.start()
    stages = [
        pltpu.make_async_copy(fresh.at[:, cols(dest * heads_own + j)], q_box.at[j - 1, dest], stage_sem.at[j - 1, dest])
        for j in range(1, heads_own)
        for dest in range(n)
    ]
    for stage in stages:
        stage.start()

    rows_load.wait()
    slot = lax.broadcasted_iota(jnp.int32, (1, tok), 1)
    live = jnp.where(slot < count_ref[0], rows_vmem[...], -1)
    hit = lax.broadcasted_iota(jnp.int32, (tok, tok), 0) == live
    edited = jnp.max(hit.astype(jnp.float32), axis=1, keepdims=True)
    mask_ref[...] = jnp.broadcast_to(edited, (tok, HEAD_DIM))

    for pair in loads:
        for load in pair:
            load.wait()

    def sent_q(j):
        for dest in peers:
            q_copy(j, dest).wait_send()

    def sent_kv(j):
        for dest in peers:
            kv_copy(j, dest).wait_send()

    out_load.start()
    send_kv(0)
    sent_q(0)
    for stage in stages:
        stage.wait()
    send_kv(1)
    sent_kv(0)
    send_q(1)

    def score(j, dest, slot):
        scores[slot] = lax.dot_general(
            q_all[j, rows(dest)],
            kv_all[j, 0],
            (((1,), (1,)), ((), ())),
            preferred_element_type=jnp.float32,
        )

    def soften(slot):
        for first in range(0, tok, CHUNK):
            piece = scores[slot, first : first + CHUNK]
            top = jnp.max(piece, axis=1, keepdims=True)
            probs[slot, first : first + CHUNK] = jnp.exp2((piece - top) * EXP2_SCALE).astype(jnp.bfloat16)

    def gather(j, dest, slot):
        values = kv_all[j, 1]
        summed = jnp.dot(
            probs[slot],
            jnp.concatenate([values, jnp.ones_like(values)], axis=1),
            preferred_element_type=jnp.float32,
        )
        o_all[j, rows(dest)] = (summed[:, :HEAD_DIM] / summed[:, HEAD_DIM:]).astype(jnp.bfloat16)

    order = peers + [me]

    def send_o(j, dest):
        if dest is me:
            o_own(j).start()
        else:
            o_copy(j, dest).start()

    def head(j, carry):
        @pl.when(j > 0)
        def _():
            sent_kv(j)

            @pl.when(j + 1 < heads_own)
            def _():
                send_kv(j + 1)

            sent_q(j)

            @pl.when(j + 1 < heads_own)
            def _():
                send_q(j + 1)

        @pl.when(j + 1 == heads_own)
        def _():
            def early(before, carry):
                for dest in order:
                    send_o(before, dest)
                return carry

            lax.fori_loop(0, heads_own - 1, early, 0)

        for dest in order:
            wait_kv(j, dest)

        for first in range(0, n, BLOCKS):
            dests = order[first : first + BLOCKS]
            for dest in dests:
                wait_q(j, dest)
            score(j, dests[0], 0)
            for index, dest in enumerate(dests):
                if index + 1 < BLOCKS:
                    score(j, dests[index + 1], (index + 1) % 2)
                soften(index % 2)
                gather(j, dest, index % 2)

            @pl.when(j + 1 == heads_own)
            def _():
                for dest in dests:
                    send_o(j, dest)

        return carry

    lax.fori_loop(0, heads_own, head, 0)

    out_load.wait()

    def drain(j, carry):
        mask = mask_ref[...] > 0.0
        for source in peers[::-1] + [me]:
            index = source * heads_own + j
            at = cols(index)
            pltpu.make_async_copy(att.at[index], att.at[index], o_recv.at[j, source]).wait()
            out_ref[:, at] = jnp.where(
                mask, att[index].astype(jnp.float32), out_ref[:, at].astype(jnp.float32)
            ).astype(jnp.bfloat16)
        for dest in peers:
            o_copy(j, dest).wait_send()
        return carry

    lax.fori_loop(0, heads_own, drain, 0)


def settle(merged, out, sems):
    slab = merged.shape[0] // SLABS
    copies = [
        pltpu.make_async_copy(merged.at[pl.ds(at * slab, slab)], out.at[pl.ds(at * slab, slab)], sems.at[at])
        for at in range(SLABS)
    ]
    for copy in copies:
        copy.start()
    for copy in copies:
        copy.wait()


def on_device(n, fresh_qkv, stale_kv, stale_out, edit_count, edit_rows):
    tok, width = stale_out.shape
    heads_own = HEADS // n
    total = tok * n
    flops = heads_own * total * total * HEAD_DIM * 4
    bf16 = jnp.bfloat16
    sems = pltpu.SemaphoreType.DMA((heads_own, n))
    merged = pl.pallas_call(
        functools.partial(kernel, n, heads_own),
        out_shape=jax.ShapeDtypeStruct((tok, width), bf16),
        in_specs=[
            pl.BlockSpec(memory_space=pltpu.SMEM),
            pl.BlockSpec(memory_space=pltpu.HBM),
            pl.BlockSpec(memory_space=pltpu.HBM),
            pl.BlockSpec(memory_space=pltpu.HBM),
            pl.BlockSpec(memory_space=pltpu.HBM),
        ],
        out_specs=pl.BlockSpec(memory_space=pltpu.VMEM),
        scratch_shapes=[
            pltpu.VMEM((HEADS, tok, HEAD_DIM), bf16),
            pltpu.VMEM((tok, HEAD_DIM), jnp.float32),
            pltpu.VMEM((tok, 2 * width), bf16),
            pltpu.VMEM((tok, 2 * width), bf16),
            pltpu.VMEM((1, tok), jnp.int32),
            pltpu.VMEM((heads_own - 1, n, tok, HEAD_DIM), bf16),
            pltpu.SemaphoreType.DMA((heads_own - 1, n)),
            pltpu.VMEM((heads_own, n, 2, tok, HEAD_DIM), bf16),
            pltpu.VMEM((heads_own, total, HEAD_DIM), bf16),
            pltpu.VMEM((heads_own, 2, total, HEAD_DIM), bf16),
            pltpu.VMEM((heads_own, total, HEAD_DIM), bf16),
            pltpu.VMEM((2, tok, total), jnp.float32),
            pltpu.VMEM((2, tok, total), bf16),
            pltpu.SemaphoreType.DMA((3, 2)),
            sems,
            sems,
            sems,
            sems,
            sems,
            sems,
        ],
        compiler_params=pltpu.CompilerParams(
            collective_id=0, has_side_effects=True, vmem_limit_bytes=48 * 1024 * 1024
        ),
        cost_estimate=pl.CostEstimate(
            flops=flops, bytes_accessed=8 * tok * width * 2, transcendentals=heads_own * total * total
        ),
    )(
        edit_count,
        pltpu.with_memory_space_constraint(edit_rows.reshape(1, tok), pltpu.HBM),
        pltpu.with_memory_space_constraint(fresh_qkv, pltpu.HBM),
        pltpu.with_memory_space_constraint(stale_kv, pltpu.HBM),
        pltpu.with_memory_space_constraint(stale_out, pltpu.HBM),
    )
    return pl.pallas_call(
        settle,
        out_shape=jax.ShapeDtypeStruct((tok, width), bf16),
        in_specs=[pl.BlockSpec(memory_space=pltpu.VMEM)],
        out_specs=pl.BlockSpec(memory_space=pltpu.HBM),
        scratch_shapes=[pltpu.SemaphoreType.DMA((SLABS,))],
        cost_estimate=pl.CostEstimate(flops=0, bytes_accessed=2 * tok * width, transcendentals=0),
    )(pltpu.with_memory_space_constraint(merged, pltpu.VMEM))


def solution(mesh):
    n = mesh.shape["sp"]
    spec = P(("img", "sp"), None)
    flat = P(("img", "sp"))
    return jax.shard_map(
        functools.partial(on_device, n),
        mesh=mesh,
        in_specs=(spec, spec, spec, flat, flat),
        out_specs=spec,
        check_vma=False,
    )
```

```python
import functools

import jax
import jax.numpy as jnp
from jax import lax
from jax.experimental import pallas as pl
from jax.experimental.pallas import tpu as pltpu
from jax.sharding import PartitionSpec as P

HEADS = 24
HEAD_DIM = 128
EXP2_SCALE = HEAD_DIM ** (-0.5) * 1.4426950408889634
RING = 4
BLOCKS = 4
CHUNK = 16
PEERS = ((1, 2), (0, 2), (1, 1), (1, 3), (0, 1), (0, 3), (1, 0))


def cols(index):
    return pl.ds(pl.multiple_of(index * HEAD_DIM, HEAD_DIM), HEAD_DIM)


def kernel(
    n,
    heads_own,
    count_ref,
    rows_ref,
    fresh,
    stale,
    stale_out,
    out_ref,
    att,
    mask_ref,
    fresh_kv,
    stale_kv,
    rows_vmem,
    q_box,
    stage_sem,
    outbox,
    q_all,
    kv_all,
    o_all,
    scores,
    probs,
    load_sem,
    q_send,
    q_recv,
    kv_send,
    kv_recv,
    o_send,
    o_recv,
):
    me = lax.axis_index("sp")
    tok = fresh.shape[0]
    width = fresh.shape[1] // 3

    def rows(index):
        return pl.ds(pl.multiple_of(index * tok, tok), tok)

    turn_of = 1 + 2 * lax.rem(lax.axis_index("img"), 2)

    def peer(step):
        over, along = step
        return lax.rem(me // RING + over, 2) * RING + lax.rem(lax.rem(me, RING) + along * turn_of, RING)

    barrier = pltpu.get_barrier_semaphore()

    for step in PEERS:
        pl.semaphore_signal(
            barrier, inc=1, device_id={"sp": peer(step)}, device_id_type=pl.DeviceIdType.MESH
        )
    rows_load = pltpu.make_async_copy(rows_ref, rows_vmem, load_sem.at[2, 0])
    rows_load.start()
    out_load = pltpu.make_async_copy(stale_out, out_ref, load_sem.at[2, 1])
    loads = []
    for part in range(2):
        at = pl.ds(part * width, width)
        loads.append(
            (
                pltpu.make_async_copy(
                    fresh.at[:, pl.ds((part + 1) * width, width)], fresh_kv.at[:, at], load_sem.at[part, 0]
                ),
                pltpu.make_async_copy(stale.at[:, at], stale_kv.at[:, at], load_sem.at[part, 1]),
            )
        )
    pl.semaphore_wait(barrier, n - 1)

    def q_source(j, dest):
        if isinstance(j, int) and j == 0:
            return fresh.at[:, cols(dest * heads_own)]
        return q_box.at[j - 1, dest]

    def q_copy(j, dest):
        return pltpu.make_async_remote_copy(
            src_ref=q_source(j, dest),
            dst_ref=q_all.at[j, rows(me)],
            send_sem=q_send.at[j, dest],
            recv_sem=q_recv.at[j, me],
            device_id={"sp": dest},
            device_id_type=pl.DeviceIdType.MESH,
        )

    def q_own(j):
        return pltpu.make_async_copy(q_source(j, me), q_all.at[j, rows(me)], q_recv.at[j, me])

    def kv_copy(j, dest):
        return pltpu.make_async_remote_copy(
            src_ref=outbox.at[j, dest],
            dst_ref=kv_all.at[j, :, rows(me)],
            send_sem=kv_send.at[j, dest],
            recv_sem=kv_recv.at[j, me],
            device_id={"sp": dest},
            device_id_type=pl.DeviceIdType.MESH,
        )

    def kv_own(j):
        return pltpu.make_async_copy(outbox.at[j, me], kv_all.at[j, :, rows(me)], kv_recv.at[j, me])

    def o_copy(j, dest):
        return pltpu.make_async_remote_copy(
            src_ref=o_all.at[j, rows(dest)],
            dst_ref=att.at[me * heads_own + j],
            send_sem=o_send.at[j, dest],
            recv_sem=o_recv.at[j, me],
            device_id={"sp": dest},
            device_id_type=pl.DeviceIdType.MESH,
        )

    def o_own(j):
        return pltpu.make_async_copy(
            o_all.at[j, rows(me)], att.at[me * heads_own + j], o_recv.at[j, me]
        )

    def send_q(j):
        for step in PEERS:
            q_copy(j, peer(step)).start()
        q_own(j).start()

    def merge(j, dest, mask):
        for part in range(2):
            at = cols(part * HEADS + dest * heads_own + j)
            outbox[j, dest, part] = jnp.where(
                mask, fresh_kv[:, at].astype(jnp.float32), stale_kv[:, at].astype(jnp.float32)
            ).astype(jnp.bfloat16)

    def send_kv(j):
        mask = mask_ref[...] > 0.0
        for step in PEERS:
            merge(j, peer(step), mask)
            kv_copy(j, peer(step)).start()
        merge(j, me, mask)
        kv_own(j).start()

    def wait_q(j, source):
        pltpu.make_async_copy(
            q_all.at[j, rows(source)], q_all.at[j, rows(source)], q_recv.at[j, source]
        ).wait()

    def wait_kv(j, source):
        pltpu.make_async_copy(
            kv_all.at[j, :, rows(source)], kv_all.at[j, :, rows(source)], kv_recv.at[j, source]
        ).wait()

    send_q(0)
    for pair in loads:
        for load in pair:
            load.start()
    stages = [
        pltpu.make_async_copy(fresh.at[:, cols(dest * heads_own + j)], q_box.at[j - 1, dest], stage_sem.at[j - 1, dest])
        for j in range(1, heads_own)
        for dest in range(n)
    ]
    for stage in stages:
        stage.start()

    rows_load.wait()
    slot = lax.broadcasted_iota(jnp.int32, (1, tok), 1)
    live = jnp.where(slot < count_ref[0], rows_vmem[...], -1)
    hit = lax.broadcasted_iota(jnp.int32, (tok, tok), 0) == live
    edited = jnp.max(hit.astype(jnp.float32), axis=1, keepdims=True)
    mask_ref[...] = jnp.broadcast_to(edited, (tok, HEAD_DIM))

    for pair in loads:
        for load in pair:
            load.wait()

    def sent_q(j):
        for step in PEERS:
            q_copy(j, peer(step)).wait_send()

    def sent_kv(j):
        for step in PEERS:
            kv_copy(j, peer(step)).wait_send()

    out_load.start()
    send_kv(0)
    sent_q(0)
    for stage in stages:
        stage.wait()
    send_kv(1)
    sent_kv(0)
    send_q(1)

    first_core = turn_of == 1

    @pl.when(first_core)
    def _():
        send_kv(heads_own - 1)
        send_q(heads_own - 1)

    def score(j, dest, slot):
        scores[slot] = lax.dot_general(
            q_all[j, rows(dest)],
            kv_all[j, 0],
            (((1,), (1,)), ((), ())),
            preferred_element_type=jnp.float32,
        )

    def soften(slot):
        for first in range(0, tok, CHUNK):
            piece = scores[slot, first : first + CHUNK]
            top = jnp.max(piece, axis=1, keepdims=True)
            probs[slot, first : first + CHUNK] = jnp.exp2((piece - top) * EXP2_SCALE).astype(jnp.bfloat16)

    def gather(j, dest, slot):
        values = kv_all[j, 1]
        summed = jnp.dot(
            probs[slot],
            jnp.concatenate([values, jnp.ones_like(values)], axis=1),
            preferred_element_type=jnp.float32,
        )
        o_all[j, rows(dest)] = (summed[:, :HEAD_DIM] / summed[:, HEAD_DIM:]).astype(jnp.bfloat16)

    order = PEERS + ((0, 0),)

    def send_o(j, step):
        if step == (0, 0):
            o_own(j).start()
        else:
            o_copy(j, peer(step)).start()

    def head(j, carry):
        @pl.when(j > 0)
        def _():
            sent_kv(j)

            @pl.when(jnp.logical_and(j + 1 < heads_own, jnp.logical_not(first_core)))
            def _():
                send_kv(j + 1)

            sent_q(j)

            @pl.when(jnp.logical_and(j + 1 < heads_own, jnp.logical_not(first_core)))
            def _():
                send_q(j + 1)

        @pl.when(j + 1 == heads_own)
        def _():
            def early(before, carry):
                for step in order:
                    send_o(before, step)
                return carry

            lax.fori_loop(0, heads_own - 1, early, 0)

        for step in order:
            wait_kv(j, peer(step))
            wait_q(j, peer(step))

        for first in range(0, n, BLOCKS):
            steps = order[first : first + BLOCKS]
            score(j, peer(steps[0]), 0)
            for index, step in enumerate(steps):
                if index + 1 < BLOCKS:
                    score(j, peer(steps[index + 1]), (index + 1) % 2)
                soften(index % 2)
                gather(j, peer(step), index % 2)

            @pl.when(j + 1 == heads_own)
            def _():
                for step in steps:
                    send_o(j, step)

        return carry

    lax.fori_loop(0, heads_own, head, 0)

    out_load.wait()

    def drain(j, carry):
        mask = mask_ref[...] > 0.0
        for step in PEERS[::-1] + ((0, 0),):
            index = peer(step) * heads_own + j
            at = cols(index)
            pltpu.make_async_copy(att.at[index], att.at[index], o_recv.at[j, peer(step)]).wait()
            out_ref[:, at] = jnp.where(
                mask, att[index].astype(jnp.float32), out_ref[:, at].astype(jnp.float32)
            ).astype(jnp.bfloat16)
        for step in PEERS:
            o_copy(j, peer(step)).wait_send()
        return carry

    lax.fori_loop(0, heads_own, drain, 0)


def on_device(n, fresh_qkv, stale_kv, stale_out, edit_count, edit_rows):
    tok, width = stale_out.shape
    heads_own = HEADS // n
    total = tok * n
    flops = heads_own * total * total * HEAD_DIM * 4
    bf16 = jnp.bfloat16
    sems = pltpu.SemaphoreType.DMA((heads_own, n))
    return pl.pallas_call(
        functools.partial(kernel, n, heads_own),
        out_shape=jax.ShapeDtypeStruct((tok, width), bf16),
        in_specs=[
            pl.BlockSpec(memory_space=pltpu.SMEM),
            pl.BlockSpec(memory_space=pltpu.HBM),
            pl.BlockSpec(memory_space=pltpu.HBM),
            pl.BlockSpec(memory_space=pltpu.HBM),
            pl.BlockSpec(memory_space=pltpu.HBM),
        ],
        out_specs=pl.BlockSpec(memory_space=pltpu.VMEM),
        scratch_shapes=[
            pltpu.VMEM((HEADS, tok, HEAD_DIM), bf16),
            pltpu.VMEM((tok, HEAD_DIM), jnp.float32),
            pltpu.VMEM((tok, 2 * width), bf16),
            pltpu.VMEM((tok, 2 * width), bf16),
            pltpu.VMEM((1, tok), jnp.int32),
            pltpu.VMEM((heads_own - 1, n, tok, HEAD_DIM), bf16),
            pltpu.SemaphoreType.DMA((heads_own - 1, n)),
            pltpu.VMEM((heads_own, n, 2, tok, HEAD_DIM), bf16),
            pltpu.VMEM((heads_own, total, HEAD_DIM), bf16),
            pltpu.VMEM((heads_own, 2, total, HEAD_DIM), bf16),
            pltpu.VMEM((heads_own, total, HEAD_DIM), bf16),
            pltpu.VMEM((2, tok, total), jnp.float32),
            pltpu.VMEM((2, tok, total), bf16),
            pltpu.SemaphoreType.DMA((3, 2)),
            sems,
            sems,
            sems,
            sems,
            sems,
            sems,
        ],
        compiler_params=pltpu.CompilerParams(
            collective_id=0, has_side_effects=True, vmem_limit_bytes=48 * 1024 * 1024
        ),
        cost_estimate=pl.CostEstimate(
            flops=flops, bytes_accessed=8 * tok * width * 2, transcendentals=heads_own * total * total
        ),
    )(
        edit_count,
        pltpu.with_memory_space_constraint(edit_rows.reshape(1, tok), pltpu.HBM),
        pltpu.with_memory_space_constraint(fresh_qkv, pltpu.HBM),
        pltpu.with_memory_space_constraint(stale_kv, pltpu.HBM),
        pltpu.with_memory_space_constraint(stale_out, pltpu.HBM),
    )


def solution(mesh):
    n = mesh.shape["sp"]
    spec = P(("img", "sp"), None)
    flat = P(("img", "sp"))
    return jax.shard_map(
        functools.partial(on_device, n),
        mesh=mesh,
        in_specs=(spec, spec, spec, flat, flat),
        out_specs=spec,
        check_vma=False,
    )
```

```python
import functools

import jax
import jax.numpy as jnp
from jax import lax
from jax.experimental import pallas as pl
from jax.experimental.pallas import tpu as pltpu
from jax.sharding import PartitionSpec as P

HEADS = 24
HEAD_DIM = 128
EXP2_SCALE = HEAD_DIM ** (-0.5) * 1.4426950408889634
RING = 4
BLOCKS = 4
CHUNK = 16
PEERS = ((1, 2), (0, 2), (1, 1), (1, 3), (0, 1), (0, 3), (1, 0))


def cols(index):
    return pl.ds(pl.multiple_of(index * HEAD_DIM, HEAD_DIM), HEAD_DIM)


def kernel(
    n,
    heads_own,
    count_ref,
    rows_ref,
    fresh,
    stale,
    stale_out,
    out_ref,
    att,
    mask_ref,
    fresh_kv,
    stale_kv,
    rows_vmem,
    q_box,
    stage_sem,
    outbox,
    q_all,
    kv_all,
    o_all,
    scores,
    probs,
    load_sem,
    q_send,
    q_recv,
    kv_send,
    kv_recv,
    o_send,
    o_recv,
):
    me = lax.axis_index("sp")
    tok = fresh.shape[0]
    width = fresh.shape[1] // 3

    def rows(index):
        return pl.ds(pl.multiple_of(index * tok, tok), tok)

    turn_of = 1 + 2 * lax.rem(lax.axis_index("img"), 2)

    def peer(step):
        over, along = step
        return lax.rem(me // RING + over, 2) * RING + lax.rem(lax.rem(me, RING) + along * turn_of, RING)

    barrier = pltpu.get_barrier_semaphore()

    for step in PEERS:
        pl.semaphore_signal(
            barrier, inc=1, device_id={"sp": peer(step)}, device_id_type=pl.DeviceIdType.MESH
        )
    rows_load = pltpu.make_async_copy(rows_ref, rows_vmem, load_sem.at[2, 0])
    rows_load.start()
    out_load = pltpu.make_async_copy(stale_out, out_ref, load_sem.at[2, 1])
    loads = []
    for part in range(2):
        at = pl.ds(part * width, width)
        loads.append(
            (
                pltpu.make_async_copy(
                    fresh.at[:, pl.ds((part + 1) * width, width)], fresh_kv.at[:, at], load_sem.at[part, 0]
                ),
                pltpu.make_async_copy(stale.at[:, at], stale_kv.at[:, at], load_sem.at[part, 1]),
            )
        )
    pl.semaphore_wait(barrier, n - 1)

    def q_source(j, dest):
        if isinstance(j, int) and j == 0:
            return fresh.at[:, cols(dest * heads_own)]
        return q_box.at[j - 1, dest]

    def q_copy(j, dest):
        return pltpu.make_async_remote_copy(
            src_ref=q_source(j, dest),
            dst_ref=q_all.at[j, rows(me)],
            send_sem=q_send.at[j, dest],
            recv_sem=q_recv.at[j, me],
            device_id={"sp": dest},
            device_id_type=pl.DeviceIdType.MESH,
        )

    def q_own(j):
        return pltpu.make_async_copy(q_source(j, me), q_all.at[j, rows(me)], q_recv.at[j, me])

    def kv_copy(j, dest):
        return pltpu.make_async_remote_copy(
            src_ref=outbox.at[j, dest],
            dst_ref=kv_all.at[j, :, rows(me)],
            send_sem=kv_send.at[j, dest],
            recv_sem=kv_recv.at[j, me],
            device_id={"sp": dest},
            device_id_type=pl.DeviceIdType.MESH,
        )

    def kv_own(j):
        return pltpu.make_async_copy(outbox.at[j, me], kv_all.at[j, :, rows(me)], kv_recv.at[j, me])

    def o_copy(j, dest):
        return pltpu.make_async_remote_copy(
            src_ref=o_all.at[j, rows(dest)],
            dst_ref=att.at[me * heads_own + j],
            send_sem=o_send.at[j, dest],
            recv_sem=o_recv.at[j, me],
            device_id={"sp": dest},
            device_id_type=pl.DeviceIdType.MESH,
        )

    def o_own(j):
        return pltpu.make_async_copy(
            o_all.at[j, rows(me)], att.at[me * heads_own + j], o_recv.at[j, me]
        )

    def send_q(j):
        for step in PEERS:
            q_copy(j, peer(step)).start()
        q_own(j).start()

    def merge(j, dest, mask):
        for part in range(2):
            at = cols(part * HEADS + dest * heads_own + j)
            outbox[j, dest, part] = jnp.where(
                mask, fresh_kv[:, at].astype(jnp.float32), stale_kv[:, at].astype(jnp.float32)
            ).astype(jnp.bfloat16)

    def send_kv(j):
        mask = mask_ref[...] > 0.0
        for step in PEERS:
            merge(j, peer(step), mask)
            kv_copy(j, peer(step)).start()
        merge(j, me, mask)
        kv_own(j).start()

    def wait_q(j, source):
        pltpu.make_async_copy(
            q_all.at[j, rows(source)], q_all.at[j, rows(source)], q_recv.at[j, source]
        ).wait()

    def wait_kv(j, source):
        pltpu.make_async_copy(
            kv_all.at[j, :, rows(source)], kv_all.at[j, :, rows(source)], kv_recv.at[j, source]
        ).wait()

    send_q(0)
    for pair in loads:
        for load in pair:
            load.start()
    stages = [
        pltpu.make_async_copy(fresh.at[:, cols(dest * heads_own + j)], q_box.at[j - 1, dest], stage_sem.at[j - 1, dest])
        for j in range(1, heads_own)
        for dest in range(n)
    ]
    for stage in stages:
        stage.start()

    rows_load.wait()
    slot = lax.broadcasted_iota(jnp.int32, (1, tok), 1)
    live = jnp.where(slot < count_ref[0], rows_vmem[...], -1)
    hit = lax.broadcasted_iota(jnp.int32, (tok, tok), 0) == live
    edited = jnp.max(hit.astype(jnp.float32), axis=1, keepdims=True)
    mask_ref[...] = jnp.broadcast_to(edited, (tok, HEAD_DIM))

    for pair in loads:
        for load in pair:
            load.wait()

    def sent_q(j):
        for step in PEERS:
            q_copy(j, peer(step)).wait_send()

    def sent_kv(j):
        for step in PEERS:
            kv_copy(j, peer(step)).wait_send()

    out_load.start()
    send_kv(0)
    sent_q(0)
    for stage in stages:
        stage.wait()
    send_kv(1)
    sent_kv(0)
    send_q(1)

    def score(j, dest, slot):
        scores[slot] = lax.dot_general(
            q_all[j, rows(dest)],
            kv_all[j, 0],
            (((1,), (1,)), ((), ())),
            preferred_element_type=jnp.float32,
        )

    def soften(slot):
        for first in range(0, tok, CHUNK):
            piece = scores[slot, first : first + CHUNK]
            top = jnp.max(piece, axis=1, keepdims=True)
            probs[slot, first : first + CHUNK] = jnp.exp2((piece - top) * EXP2_SCALE).astype(jnp.bfloat16)

    def gather(j, dest, slot):
        values = kv_all[j, 1]
        summed = jnp.dot(
            probs[slot],
            jnp.concatenate([values, jnp.ones_like(values)], axis=1),
            preferred_element_type=jnp.float32,
        )
        o_all[j, rows(dest)] = (summed[:, :HEAD_DIM] / summed[:, HEAD_DIM:]).astype(jnp.bfloat16)

    order = PEERS + ((0, 0),)

    def send_o(j, step):
        if step == (0, 0):
            o_own(j).start()
        else:
            o_copy(j, peer(step)).start()

    def head(j, carry):
        @pl.when(j + 1 == heads_own)
        def _():
            def early(before, carry):
                for step in order:
                    send_o(before, step)
                return carry

            lax.fori_loop(0, heads_own - 1, early, 0)

        @pl.when(j > 0)
        def _():
            sent_kv(j)

            @pl.when(j + 1 < heads_own)
            def _():
                send_kv(j + 1)

            sent_q(j)

            @pl.when(j + 1 < heads_own)
            def _():
                send_q(j + 1)

        for step in order:
            wait_kv(j, peer(step))
            wait_q(j, peer(step))

        for first in range(0, n, BLOCKS):
            steps = order[first : first + BLOCKS]
            score(j, peer(steps[0]), 0)
            for index, step in enumerate(steps):
                if index + 1 < BLOCKS:
                    score(j, peer(steps[index + 1]), (index + 1) % 2)
                soften(index % 2)
                gather(j, peer(step), index % 2)

            @pl.when(j + 1 == heads_own)
            def _():
                for step in steps:
                    send_o(j, step)

        return carry

    lax.fori_loop(0, heads_own, head, 0)

    out_load.wait()

    def drain(j, carry):
        mask = mask_ref[...] > 0.0
        for step in PEERS[::-1] + ((0, 0),):
            index = peer(step) * heads_own + j
            at = cols(index)
            pltpu.make_async_copy(att.at[index], att.at[index], o_recv.at[j, peer(step)]).wait()
            out_ref[:, at] = jnp.where(
                mask, att[index].astype(jnp.float32), out_ref[:, at].astype(jnp.float32)
            ).astype(jnp.bfloat16)
        for step in PEERS:
            o_copy(j, peer(step)).wait_send()
        return carry

    lax.fori_loop(0, heads_own, drain, 0)


def on_device(n, fresh_qkv, stale_kv, stale_out, edit_count, edit_rows):
    tok, width = stale_out.shape
    heads_own = HEADS // n
    total = tok * n
    flops = heads_own * total * total * HEAD_DIM * 4
    bf16 = jnp.bfloat16
    sems = pltpu.SemaphoreType.DMA((heads_own, n))
    return pl.pallas_call(
        functools.partial(kernel, n, heads_own),
        out_shape=jax.ShapeDtypeStruct((tok, width), bf16),
        in_specs=[
            pl.BlockSpec(memory_space=pltpu.SMEM),
            pl.BlockSpec(memory_space=pltpu.HBM),
            pl.BlockSpec(memory_space=pltpu.HBM),
            pl.BlockSpec(memory_space=pltpu.HBM),
            pl.BlockSpec(memory_space=pltpu.HBM),
        ],
        out_specs=pl.BlockSpec(memory_space=pltpu.VMEM),
        scratch_shapes=[
            pltpu.VMEM((HEADS, tok, HEAD_DIM), bf16),
            pltpu.VMEM((tok, HEAD_DIM), jnp.float32),
            pltpu.VMEM((tok, 2 * width), bf16),
            pltpu.VMEM((tok, 2 * width), bf16),
            pltpu.VMEM((1, tok), jnp.int32),
            pltpu.VMEM((heads_own - 1, n, tok, HEAD_DIM), bf16),
            pltpu.SemaphoreType.DMA((heads_own - 1, n)),
            pltpu.VMEM((heads_own, n, 2, tok, HEAD_DIM), bf16),
            pltpu.VMEM((heads_own, total, HEAD_DIM), bf16),
            pltpu.VMEM((heads_own, 2, total, HEAD_DIM), bf16),
            pltpu.VMEM((heads_own, total, HEAD_DIM), bf16),
            pltpu.VMEM((2, tok, total), jnp.float32),
            pltpu.VMEM((2, tok, total), bf16),
            pltpu.SemaphoreType.DMA((3, 2)),
            sems,
            sems,
            sems,
            sems,
            sems,
            sems,
        ],
        compiler_params=pltpu.CompilerParams(
            collective_id=0, has_side_effects=True, vmem_limit_bytes=48 * 1024 * 1024
        ),
        cost_estimate=pl.CostEstimate(
            flops=flops, bytes_accessed=8 * tok * width * 2, transcendentals=heads_own * total * total
        ),
    )(
        edit_count,
        pltpu.with_memory_space_constraint(edit_rows.reshape(1, tok), pltpu.HBM),
        pltpu.with_memory_space_constraint(fresh_qkv, pltpu.HBM),
        pltpu.with_memory_space_constraint(stale_kv, pltpu.HBM),
        pltpu.with_memory_space_constraint(stale_out, pltpu.HBM),
    )


def solution(mesh):
    n = mesh.shape["sp"]
    spec = P(("img", "sp"), None)
    flat = P(("img", "sp"))
    return jax.shard_map(
        functools.partial(on_device, n),
        mesh=mesh,
        in_specs=(spec, spec, spec, flat, flat),
        out_specs=spec,
        check_vma=False,
    )
```
